32 devices in a mesh: dp: 4 (over y, x), seq: 4 (over z), tensor: 2 (over core).
Axes of the slice: x: 2, y: 2, z: 4, core: 2. Of those that a mesh axis runs over, the one named last changes fastest.
Arguments:
- clips: bfloat16 [16, 8, 192, 768], P('dp', 'seq'), may hold values from -6 to 6
- cotangent: bfloat16 [16, 8, 192, 768], P('dp', 'seq'), may hold values from -6 to 6
- clip_counts: int32 [4], P('dp'), may hold values from 1 to 4, as said below
- norm_params: float32 [6, 768], replicated, may hold values from -0.6 to 1.5
- norm_moment: float32 [6, 768], replicated, may hold values from 737.28 to 14745.6
- qkv_weight: float32 [2, 3, 768, 768], P(None, None, ('dp', 'seq'), 'tensor'), may hold values from -0.21875 to 0.21875
- qkv_row: float32 [2, 3, 768], P(None, None, ('dp', 'seq')), may hold values from 737.28 to 14745.6
- qkv_col: float32 [2, 3, 768], P(None, None, 'tensor'), may hold values from 737.28 to 14745.6
- out_weight: float32 [2, 768, 768], P(None, ('dp', 'seq'), 'tensor'), may hold values from -0.875 to 0.875
- out_row: float32 [2, 768], P(None, ('dp', 'seq')), may hold values from 737.28 to 14745.6
- out_col: float32 [2, 768], P(None, 'tensor'), may hold values from 737.28 to 14745.6
- ffn_weight: float32 [2, 768, 3072], P(None, ('dp', 'seq'), 'tensor'), may hold values from -0.21875 to 0.21875
- ffn_row: float32 [2, 768], P(None, ('dp', 'seq')), may hold values from 737.28 to 14745.6
- ffn_col: float32 [2, 3072], P(None, 'tensor'), may hold values from 737.28 to 14745.6
Outputs:
- layer_out: bfloat16 [16, 8, 192, 768], P('dp', 'seq')
- grad_input: float32 [16, 8, 192, 768], P('dp', 'seq')
- norm_grad: float32 [6, 768], replicated
- norm_moment_new: float32 [6, 768], replicated
- norm_new: float32 [6, 768], replicated
- qkv_grad: float32 [2, 3, 768, 768], P(None, None, ('dp', 'seq'), 'tensor')
- qkv_new: float32 [2, 3, 768, 768], P(None, None, ('dp', 'seq'), 'tensor')
- qkv_row_new: float32 [2, 3, 768], P(None, None, ('dp', 'seq'))
- qkv_col_new: float32 [2, 3, 768], P(None, None, 'tensor')
- out_grad: float32 [2, 768, 768], P(None, ('dp', 'seq'), 'tensor')
- out_new: float32 [2, 768, 768], P(None, ('dp', 'seq'), 'tensor')
- out_row_new: float32 [2, 768], P(None, ('dp', 'seq'))
- out_col_new: float32 [2, 768], P(None, 'tensor')
- ffn_grad: float32 [2, 768, 3072], P(None, ('dp', 'seq'), 'tensor')
- ffn_new: float32 [2, 768, 3072], P(None, ('dp', 'seq'), 'tensor')
- ffn_row_new: float32 [2, 768], P(None, ('dp', 'seq'))
- ffn_col_new: float32 [2, 3072], P(None, 'tensor')
The draws below stay inside these ranges and needn't reach their ends.
Inputs may be any that keep to these rules, and one draw needn't show every extreme that they name: `clip_counts`: in every draw some data group is full (4 clips) and another holds one clip.
All inputs are finite; a program needn't handle non-finite values.
Results may differ from the reference program's by a relative error of at most 0.017.
The reference program's roundings to bfloat16 on the way count: a program that leaves them out, or rounds other values in their place, can miss the bound.
Values may be sent and summed in bfloat16 or wider, within the bound.
A program may use at most 256 MiB of HBM per device.

```python
import math
import jax
import jax.numpy as jnp
from jax import lax

D = 768
HEADS = 12
HEAD_DIM = 64
FF = 3072
FRAMES = 8
PATCHES = 192
SLOTS = 4
STEP = 8
CLIPS = 16
N_DP = 4


def draw_clip_counts(key, part):
    key = jax.random.fold_in(key, 5)
    keys = jax.random.split(key, 3)
    counts = jax.random.randint(keys[0], (N_DP,), 1, SLOTS + 1)
    full_at = jax.random.randint(keys[1], (), 0, N_DP)
    offset = jax.random.randint(keys[2], (), 1, N_DP)
    single_at = (full_at + offset) % N_DP
    counts = counts.at[full_at].set(SLOTS).at[single_at].set(1)
    return counts.astype(jnp.int32)


def draw_norm_params(key, part):
    key = jax.random.fold_in(key, 11)
    gain_key, bias_key = jax.random.split(key)
    gains = jax.random.uniform(gain_key, (3, D), jnp.float32, 0.7, 1.3)
    biases = 0.2 * jax.random.truncated_normal(bias_key, -3.0, 3.0, (3, D), jnp.float32)
    return jnp.concatenate([gains, biases], 0)


def shard_levels(key, dims, shards, smallest, largest):
    loudness = 1.0
    for dim, blocks in shards:
        draws = jax.random.uniform(jax.random.fold_in(jax.random.fold_in(key, 6), dim), (blocks,), jnp.float32, smallest / len(shards), largest / len(shards))
        loudness = loudness * jnp.repeat(jnp.exp(draws), dims[dim] // blocks).reshape((-1,) + (1,) * (len(dims) - 1 - dim))
    return loudness


def scatter_about(key, extent, width, most, pieces=(), kind=jnp.bfloat16):
    level = shard_levels(key, extent, pieces, -0.22, 0.18) if pieces else 1.0
    values = jax.random.normal(key, extent, jnp.float32) * width * level
    return jnp.minimum(jnp.maximum(values, -most), most).astype(kind)


def setup_inputs(seed: int = 0) -> dict:
    key_list = jax.random.split(jax.random.key(seed), 15)
    clips = scatter_about(key_list[0], (CLIPS, FRAMES, PATCHES, D), 1.0, 6.0, ((0, 4), (1, 4)))
    cotangent = scatter_about(key_list[1], (CLIPS, FRAMES, PATCHES, D), 1.0, 6.0, ((0, 4), (1, 4)))
    clip_counts = draw_clip_counts(jax.random.fold_in(key_list[14], 71), 0)
    norm_params = draw_norm_params(jax.random.fold_in(key_list[14], 71), 0)
    norm_moment = jnp.clip(jnp.exp(jax.random.uniform(key_list[4], (6, D), jnp.float32, math.log(737.28), math.log(14745.6))), 737.28, 14745.6)
    qkv_weight = scatter_about(key_list[5], (2, 3, D, D), D ** -0.5, 0.21875, ((2, 16), (3, 2)), jnp.float32)
    qkv_row = jnp.clip(jnp.exp(math.log(14745.6) - 2.9957322 * jax.random.uniform(key_list[6], (2, 3, D), jnp.float32) ** shard_levels(key_list[6], (2, 3, D), ((2, 16),), -0.2, 0.2)), 737.28, 14745.6)
    qkv_col = jnp.clip(jnp.exp(math.log(14745.6) - 2.9957322 * jax.random.uniform(key_list[7], (2, 3, D), jnp.float32) ** shard_levels(key_list[7], (2, 3, D), ((2, 2),), -0.2, 0.2)), 737.28, 14745.6)
    out_weight = scatter_about(key_list[8], (2, D, D), (D // 16) ** -0.5, 0.875, ((1, 16), (2, 2)), jnp.float32)
    out_row = jnp.clip(jnp.exp(math.log(14745.6) - 2.9957322 * jax.random.uniform(key_list[9], (2, D), jnp.float32) ** shard_levels(key_list[9], (2, D), ((1, 16),), -0.2, 0.2)), 737.28, 14745.6)
    out_col = jnp.clip(jnp.exp(math.log(14745.6) - 2.9957322 * jax.random.uniform(key_list[10], (2, D), jnp.float32) ** shard_levels(key_list[10], (2, D), ((1, 2),), -0.2, 0.2)), 737.28, 14745.6)
    ffn_weight = scatter_about(key_list[11], (2, D, FF), D ** -0.5, 0.21875, ((1, 16), (2, 2)), jnp.float32)
    ffn_row = jnp.clip(jnp.exp(math.log(14745.6) - 2.9957322 * jax.random.uniform(key_list[12], (2, D), jnp.float32) ** shard_levels(key_list[12], (2, D), ((1, 16),), -0.2, 0.2)), 737.28, 14745.6)
    ffn_col = jnp.clip(jnp.exp(math.log(14745.6) - 2.9957322 * jax.random.uniform(key_list[13], (2, FF), jnp.float32) ** shard_levels(key_list[13], (2, FF), ((1, 2),), -0.2, 0.2)), 737.28, 14745.6)
    return dict(clips=clips, cotangent=cotangent, clip_counts=clip_counts, norm_params=norm_params, norm_moment=norm_moment, qkv_weight=qkv_weight, qkv_row=qkv_row, qkv_col=qkv_col, out_weight=out_weight, out_row=out_row, out_col=out_col, ffn_weight=ffn_weight, ffn_row=ffn_row, ffn_col=ffn_col)


EPS = 1e-06
EPS_ONE = 1e-30
SCALE = 0.125
RATE_QKV = 0.02
RATE_OUT = 0.07
RATE_NORM = 0.25
HIGH = lax.Precision.HIGHEST

@jax.custom_vjp
def low(v):
    return lax.optimization_barrier(v.astype(jnp.bfloat16)).astype(jnp.float32)

@jax.custom_vjp
def low_back(v):
    return v

def low_keep(v):
    return (low(v), None)

def low_pass(kept, grad):
    return (grad,)

def back_keep(v):
    return (v, None)

def back_low(kept, grad):
    return (low(grad),)
low.defvjp(low_keep, low_pass)
low_back.defvjp(back_keep, back_low)

def low_both(values):
    return low_back(low(values))

def layer_norm(values, gain_vec, bias_vec):
    centred = values - lax.optimization_barrier(jnp.mean(values, -1, keepdims=True))
    variance = lax.optimization_barrier(jnp.mean(centred * centred, -1, keepdims=True))
    return centred * lax.rsqrt(variance + EPS) * gain_vec + bias_vec

def split_heads(values):
    return values.reshape(values.shape[:-1] + (HEADS, HEAD_DIM))

def join_heads(values):
    return values.reshape(values.shape[:-2] + (HEADS * HEAD_DIM,))

def attention(query_part, key_part, value_part, score_form, mix_form):
    scores = low_back(jnp.einsum(score_form, query_part, key_part, precision=HIGH) * SCALE)
    row_top = lax.optimization_barrier(jnp.max(scores, -1, keepdims=True))
    exp_scores = jnp.exp(scores - row_top)
    soft_weights = low(exp_scores / lax.optimization_barrier(jnp.sum(exp_scores, -1, keepdims=True)))
    return jnp.einsum(mix_form, soft_weights, value_part, precision=HIGH)

def layer_block(qkv_weight, out_weight, ffn_weight, norm_params, inputs):
    proj_low = low(qkv_weight)
    out_low = low(out_weight)
    ffn_low = low(ffn_weight)

    def branch(running, which, score_form, mix_form):
        normed = low(layer_norm(running, norm_params[which], norm_params[3 + which]))
        stacked = low_both(jnp.einsum('fpd,sde->sfpe', normed, proj_low[which], precision=HIGH))
        mixed = attention(split_heads(stacked[0]), split_heads(stacked[1]), split_heads(stacked[2]), score_form, mix_form)
        mixed = low_both(join_heads(mixed))
        return low_back(jnp.einsum('fpe,de->fpd', mixed, out_low[which], precision=HIGH))
    first = inputs + branch(inputs, 0, 'fphd,gphd->phfg', 'phfg,gphd->fphd')
    second = first + branch(first, 1, 'fphd,fkhd->fhpk', 'fhpk,fkhd->fphd')
    normed = low(layer_norm(second, norm_params[2], norm_params[5]))
    hidden = low_back(jnp.einsum('fpd,dm->fpm', normed, ffn_low[0], precision=HIGH))
    active = low(jax.nn.gelu(hidden, approximate=False))
    return second + low_back(jnp.einsum('fpm,dm->fpd', active, ffn_low[1], precision=HIGH))

def factored(grad_mat, weight, row_state, col_state, step_rate):
    decay_rate = 1.0 - STEP ** (-0.8)
    squares = grad_mat * grad_mat + EPS_ONE
    row_new = decay_rate * row_state + (1.0 - decay_rate) * lax.optimization_barrier(jnp.mean(squares, -1))
    col_new = decay_rate * col_state + (1.0 - decay_rate) * lax.optimization_barrier(jnp.mean(squares, -2))
    row_mean = lax.optimization_barrier(jnp.mean(row_new, -1))
    second = row_new[..., :, None] * col_new[..., None, :] / row_mean[..., None, None]
    update = grad_mat * lax.rsqrt(second)
    return (weight - step_rate * update, row_new, col_new)

def reference(clips, cotangent, clip_counts, norm_params, norm_moment, qkv_weight, qkv_row, qkv_col, out_weight, out_row, out_col, ffn_weight, ffn_row, ffn_col):
    clip_index = jnp.arange(CLIPS, dtype=jnp.int32)
    group_index = clip_index // SLOTS
    alive_mask = (clip_index - group_index * SLOTS < clip_counts[group_index]).astype(jnp.float32)
    params = (qkv_weight, out_weight, ffn_weight, norm_params)

    def forward(param_set, inputs):
        return layer_block(param_set[0], param_set[1], param_set[2], param_set[3], inputs)

    def one_clip(totals, clip_item):
        inputs, upstream, alive_one = clip_item
        result, pullback = jax.vjp(forward, params, inputs.astype(jnp.float32))
        grads, grad_in = pullback(upstream.astype(jnp.float32) * alive_one)
        totals = jax.tree.map(jnp.add, totals, grads)
        return (totals, (result.astype(jnp.bfloat16), grad_in))
    start_sum = jax.tree.map(jnp.zeros_like, params)
    totals, (layer_out, grad_input) = lax.scan(one_clip, start_sum, (clips, cotangent, alive_mask))
    qkv_grad, out_grad, ffn_grad, norm_grad = totals
    qkv_new, qkv_row_new, qkv_col_new = factored(qkv_grad, qkv_weight, qkv_row, qkv_col, RATE_QKV)
    out_new, out_row_new, out_col_new = factored(out_grad, out_weight, out_row, out_col, RATE_OUT)
    ffn_rates = jnp.array([0.02, 0.01], jnp.float32).reshape(2, 1, 1)
    ffn_new, ffn_row_new, ffn_col_new = factored(ffn_grad, ffn_weight, ffn_row, ffn_col, ffn_rates)
    decay_rate = 1.0 - STEP ** (-0.8)
    norm_moment_new = decay_rate * norm_moment + (1.0 - decay_rate) * (norm_grad * norm_grad + EPS_ONE)
    update = norm_grad * lax.rsqrt(norm_moment_new)
    update_rms = jnp.sqrt(lax.optimization_barrier(jnp.mean(update * update, -1, keepdims=True)))
    norm_new = norm_params - RATE_NORM * update / jnp.maximum(1.0, update_rms)
    return (layer_out, grad_input, norm_grad, norm_moment_new, norm_new, qkv_grad, qkv_new, qkv_row_new, qkv_col_new, out_grad, out_new, out_row_new, out_col_new, ffn_grad, ffn_new, ffn_row_new, ffn_col_new)
```

```python
import jax
import jax.numpy as jnp
from jax import lax
from jax.experimental import pallas as pl
from jax.experimental.pallas import tpu as pltpu
from jax.sharding import PartitionSpec as P

HEAD_DIM = 64
MICRO = 2
STEP = 8


EPS = 1e-06
EPS_ONE = 1e-30
SCALE = 0.125
RATE_QKV = 0.02
RATE_OUT = 0.07
RATE_NORM = 0.25
TEMPORAL = ("cfphd", "cgphd", "cphfg")
SPATIAL = ("cfphd", "cfkhd", "cfhpk")


def layer_norm(values, gain_vec, bias_vec):
    centred = values - jnp.mean(values, -1, keepdims=True)
    variance = jnp.mean(centred * centred, -1, keepdims=True)
    return centred * lax.rsqrt(variance + EPS) * gain_vec + bias_vec


def norm_back(values, gain_vec, bias_vec, upstream):
    unused, pullback = jax.vjp(layer_norm, values, gain_vec, bias_vec)
    return pullback(upstream)


def gelu_exact(values):
    return jax.nn.gelu(values, approximate=False)


def form_pair(first, second, target):
    return first + "," + second + "->" + target


def split_heads(piece):
    return piece.reshape(piece.shape[:-1] + (piece.shape[-1] // HEAD_DIM, HEAD_DIM))


def join_heads(values):
    return values.reshape(values.shape[:-2] + (values.shape[-2] * values.shape[-1],))


def to_places(stacked):
    return lax.all_to_all(stacked, "seq", split_axis=3, concat_axis=2, tiled=True)


def to_frames(stacked):
    return lax.all_to_all(stacked, "seq", split_axis=2, concat_axis=3, tiled=True)


def tensor_total(partial_term):
    return lax.psum(partial_term, "tensor")


def attend(stacked, form_set):
    q_form, k_form, s_form = form_set
    query_part = split_heads(stacked[0])
    key_part = split_heads(stacked[1])
    value_part = split_heads(stacked[2])
    scores = (
        jnp.einsum(
            form_pair(q_form, k_form, s_form),
            query_part,
            key_part,
            preferred_element_type=jnp.float32,
        )
        * SCALE
    )
    row_top = jnp.max(scores, -1, keepdims=True)
    exp_scores = jnp.exp(scores - row_top)
    denom_sum = jnp.sum(exp_scores, -1, keepdims=True)
    soft_weights = (exp_scores / denom_sum).astype(jnp.bfloat16)
    mixed = jnp.einsum(
        form_pair(s_form, k_form, q_form),
        soft_weights,
        value_part,
        preferred_element_type=jnp.float32,
    )
    return (join_heads(mixed).astype(jnp.bfloat16), row_top + jnp.log(denom_sum))


def attend_back(stacked, log_total, grad_mixed, form_set):
    q_form, k_form, s_form = form_set
    query_part = split_heads(stacked[0])
    key_part = split_heads(stacked[1])
    value_part = split_heads(stacked[2])
    grad_heads = split_heads(grad_mixed)
    scores = (
        jnp.einsum(
            form_pair(q_form, k_form, s_form),
            query_part,
            key_part,
            preferred_element_type=jnp.float32,
        )
        * SCALE
    )
    soft_full = jnp.exp(scores - log_total)
    grad_soft = jnp.einsum(
        form_pair(q_form, k_form, s_form),
        grad_heads,
        value_part,
        preferred_element_type=jnp.float32,
    )
    centre = jnp.sum(soft_full * grad_soft, -1, keepdims=True)
    grad_scores = (soft_full * (grad_soft - centre)).astype(jnp.bfloat16)
    grad_query = (
        jnp.einsum(
            form_pair(s_form, k_form, q_form),
            grad_scores,
            key_part,
            preferred_element_type=jnp.float32,
        )
        * SCALE
    ).astype(jnp.bfloat16)
    grad_key = (
        jnp.einsum(
            form_pair(s_form, q_form, k_form),
            grad_scores,
            query_part,
            preferred_element_type=jnp.float32,
        )
        * SCALE
    ).astype(jnp.bfloat16)
    grad_value = jnp.einsum(
        form_pair(s_form, q_form, k_form),
        soft_full.astype(jnp.bfloat16),
        grad_heads,
        preferred_element_type=jnp.float32,
    ).astype(jnp.bfloat16)
    return jnp.stack([join_heads(grad_query), join_heads(grad_key), join_heads(grad_value)])


def micro_step(inputs_low, upstream_low, alive_part, gathered, norm_params):
    proj_w, out_w, ffn_w = gathered
    inputs = inputs_low.astype(jnp.float32)
    normed_one = layer_norm(inputs, norm_params[0], norm_params[3]).astype(jnp.bfloat16)
    qkv_one = jnp.einsum(
        "cfpd,sde->scfpe", normed_one, proj_w[0], preferred_element_type=jnp.float32
    ).astype(jnp.bfloat16)
    places = to_places(qkv_one)
    mixed_places, log_one = attend(places, TEMPORAL)
    mixed_one = to_frames(mixed_places[None])[0]
    first = inputs + tensor_total(
        jnp.einsum("cfpe,de->cfpd", mixed_one, out_w[0], preferred_element_type=jnp.float32)
    )
    normed_two = layer_norm(first, norm_params[1], norm_params[4]).astype(jnp.bfloat16)
    qkv_two = jnp.einsum(
        "cfpd,sde->scfpe", normed_two, proj_w[1], preferred_element_type=jnp.float32
    ).astype(jnp.bfloat16)
    mixed_two, log_two = attend(qkv_two, SPATIAL)
    second = first + tensor_total(
        jnp.einsum("cfpe,de->cfpd", mixed_two, out_w[1], preferred_element_type=jnp.float32)
    )
    normed_three = layer_norm(second, norm_params[2], norm_params[5]).astype(jnp.bfloat16)
    hidden = jnp.einsum("cfpd,dm->cfpm", normed_three, ffn_w[0], preferred_element_type=jnp.float32)
    active_full, gelu_pull = jax.vjp(gelu_exact, hidden)
    active = active_full.astype(jnp.bfloat16)
    result = second + tensor_total(
        jnp.einsum("cfpm,dm->cfpd", active, ffn_w[1], preferred_element_type=jnp.float32)
    )
    upstream = upstream_low.astype(jnp.float32) * alive_part[:, None, None, None]
    grad_low = upstream.astype(jnp.bfloat16)
    grad_ffn_out = jnp.einsum("cfpd,cfpm->dm", grad_low, active, preferred_element_type=jnp.float32)
    grad_active = jnp.einsum(
        "cfpd,dm->cfpm", grad_low, ffn_w[1], preferred_element_type=jnp.float32
    )
    grad_hidden = gelu_pull(grad_active)[0].astype(jnp.bfloat16)
    grad_ffn_in = jnp.einsum(
        "cfpd,cfpm->dm", normed_three, grad_hidden, preferred_element_type=jnp.float32
    )
    grad_normed = tensor_total(
        jnp.einsum("cfpm,dm->cfpd", grad_hidden, ffn_w[0], preferred_element_type=jnp.float32)
    )
    back_three, gain_three, bias_three = norm_back(
        second, norm_params[2], norm_params[5], grad_normed
    )
    upstream = upstream + back_three
    grad_low = upstream.astype(jnp.bfloat16)
    grad_out_two = jnp.einsum(
        "cfpd,cfpe->de", grad_low, mixed_two, preferred_element_type=jnp.float32
    )
    grad_mixed_two = jnp.einsum(
        "cfpd,de->cfpe", grad_low, out_w[1], preferred_element_type=jnp.float32
    ).astype(jnp.bfloat16)
    grad_qkv_two = attend_back(qkv_two, log_two, grad_mixed_two, SPATIAL)
    grad_proj_two = jnp.einsum(
        "cfpd,scfpe->sde", normed_two, grad_qkv_two, preferred_element_type=jnp.float32
    )
    grad_normed = tensor_total(
        jnp.einsum("scfpe,sde->cfpd", grad_qkv_two, proj_w[1], preferred_element_type=jnp.float32)
    )
    back_two, gain_two, bias_two = norm_back(first, norm_params[1], norm_params[4], grad_normed)
    upstream = upstream + back_two
    grad_low = upstream.astype(jnp.bfloat16)
    grad_out_one = jnp.einsum(
        "cfpd,cfpe->de", grad_low, mixed_one, preferred_element_type=jnp.float32
    )
    grad_mixed_one = jnp.einsum(
        "cfpd,de->cfpe", grad_low, out_w[0], preferred_element_type=jnp.float32
    ).astype(jnp.bfloat16)
    grad_places = attend_back(places, log_one, to_places(grad_mixed_one[None])[0], TEMPORAL)
    grad_qkv_one = to_frames(grad_places)
    grad_proj_one = jnp.einsum(
        "cfpd,scfpe->sde", normed_one, grad_qkv_one, preferred_element_type=jnp.float32
    )
    grad_normed = tensor_total(
        jnp.einsum("scfpe,sde->cfpd", grad_qkv_one, proj_w[0], preferred_element_type=jnp.float32)
    )
    back_one, gain_one, bias_one = norm_back(inputs, norm_params[0], norm_params[3], grad_normed)
    upstream = upstream + back_one
    weight_grads = (
        jnp.stack([grad_proj_one, grad_proj_two]),
        jnp.stack([grad_out_one, grad_out_two]),
        jnp.stack([grad_ffn_in, grad_ffn_out]),
    )
    norm_grads = jnp.stack([gain_one, gain_two, gain_three, bias_one, bias_two, bias_three])
    return (result.astype(jnp.bfloat16), upstream, weight_grads, norm_grads)


def per_device(
    clips,
    cotangent,
    clip_counts,
    norm_params,
    norm_moment,
    qkv_weight,
    qkv_row,
    qkv_col,
    out_weight,
    out_row,
    out_col,
    ffn_weight,
    ffn_row,
    ffn_col,
):
    slot_count = clips.shape[0]
    per_batch = slot_count // MICRO
    model_width = clips.shape[3]
    decay_rate = 1.0 - STEP ** (-0.8)
    live_count = clip_counts[0]
    alive_mask = (jnp.arange(slot_count, dtype=jnp.int32) < live_count).astype(jnp.float32)
    shards = (
        qkv_weight.astype(jnp.bfloat16),
        out_weight.astype(jnp.bfloat16),
        ffn_weight.astype(jnp.bfloat16),
    )
    reduced = (jnp.zeros_like(qkv_weight), jnp.zeros_like(out_weight), jnp.zeros_like(ffn_weight))
    norm_sum = jnp.zeros_like(norm_params)
    results = []
    input_grads = []
    for micro_index in range(MICRO):
        lower = micro_index * per_batch
        gathered = (
            lax.all_gather(shards[0], ("dp", "seq"), axis=2, tiled=True),
            lax.all_gather(shards[1], ("dp", "seq"), axis=1, tiled=True),
            lax.all_gather(shards[2], ("dp", "seq"), axis=1, tiled=True),
        )
        result, grad_in, weight_grads, norm_grads = micro_step(
            clips[lower : lower + per_batch],
            cotangent[lower : lower + per_batch],
            alive_mask[lower : lower + per_batch],
            gathered,
            norm_params,
        )
        results.append(result)
        input_grads.append(grad_in)
        norm_sum = norm_sum + norm_grads
        pieces = (
            lax.psum_scatter(weight_grads[0], ("dp", "seq"), scatter_dimension=2, tiled=True),
            lax.psum_scatter(weight_grads[1], ("dp", "seq"), scatter_dimension=1, tiled=True),
            lax.psum_scatter(weight_grads[2], ("dp", "seq"), scatter_dimension=1, tiled=True),
        )
        reduced = jax.tree.map(jnp.add, reduced, pieces)
    weights_old = (qkv_weight, out_weight, ffn_weight)
    row_states = (qkv_row, out_row, ffn_row)
    col_states = (qkv_col, out_col, ffn_col)
    squares = [grad_mat * grad_mat + EPS_ONE for grad_mat in reduced]
    row_part = [jnp.sum(square_mat, -1) for square_mat in squares]
    total_part = [jnp.sum(square_mat, (-2, -1)) for square_mat in squares]
    section_one = lax.psum(
        (row_part[0], row_part[1], row_part[2], total_part[0], total_part[1], total_part[2]),
        "tensor",
    )
    col_part = [jnp.sum(square_mat, -2) for square_mat in squares]
    old_part = [jnp.sum(row_state, -1) for row_state in row_states]
    section_two = lax.psum(
        (
            col_part[0],
            col_part[1],
            col_part[2],
            section_one[3],
            section_one[4],
            section_one[5],
            old_part[0],
            old_part[1],
            old_part[2],
            norm_sum,
        ),
        ("dp", "seq"),
    )
    norm_grad = section_two[9]
    tensor_ways = lax.axis_size("tensor")
    rates = (
        jnp.float32(RATE_QKV),
        jnp.float32(RATE_OUT),
        jnp.array([0.02, 0.01], jnp.float32).reshape(2, 1, 1),
    )
    new_weights = []
    row_news = []
    col_news = []
    for which in range(3):
        columns_all = reduced[which].shape[-1] * tensor_ways
        row_new = (
            decay_rate * row_states[which] + (1.0 - decay_rate) * section_one[which] / columns_all
        )
        col_new = (
            decay_rate * col_states[which] + (1.0 - decay_rate) * section_two[which] / model_width
        )
        row_mean = decay_rate * section_two[6 + which] / model_width + (
            1.0 - decay_rate
        ) * section_two[3 + which] / (model_width * columns_all)
        second = row_new[..., :, None] * col_new[..., None, :] / row_mean[..., None, None]
        update = reduced[which] * lax.rsqrt(second)
        new_weights.append(weights_old[which] - rates[which] * update)
        row_news.append(row_new)
        col_news.append(col_new)
    norm_moment_new = decay_rate * norm_moment + (1.0 - decay_rate) * (
        norm_grad * norm_grad + EPS_ONE
    )
    norm_update = norm_grad * lax.rsqrt(norm_moment_new)
    norm_rms = jnp.sqrt(jnp.mean(norm_update * norm_update, -1, keepdims=True))
    norm_new = norm_params - RATE_NORM * norm_update / jnp.maximum(1.0, norm_rms)
    layer_out = jnp.concatenate(results, 0)
    grad_input = jnp.concatenate(input_grads, 0)
    return (
        layer_out,
        grad_input,
        norm_grad,
        norm_moment_new,
        norm_new,
        reduced[0],
        new_weights[0],
        row_news[0],
        col_news[0],
        reduced[1],
        new_weights[1],
        row_news[1],
        col_news[1],
        reduced[2],
        new_weights[2],
        row_news[2],
        col_news[2],
    )


MESH_ID = pl.DeviceIdType.MESH
BF = jnp.bfloat16
F32 = jnp.float32
NEG = -1e30
SQRT_HALF = 0.7071067811865476
INV_SQRT_2PI = 0.3989422804014327


def nn(a, b):
    return lax.dot_general(a, b, (((1,), (0,)), ((), ())), preferred_element_type=F32)


def nt(a, b):
    return lax.dot_general(a, b, (((1,), (1,)), ((), ())), preferred_element_type=F32)


def tn(a, b):
    return lax.dot_general(a, b, (((0,), (0,)), ((), ())), preferred_element_type=F32)


def flat(values):
    return values.reshape(-1, values.shape[-1])


def ln_stats(v):
    centred = v - jnp.mean(v, -1, keepdims=True)
    rstd = lax.rsqrt(jnp.mean(centred * centred, -1, keepdims=True) + EPS)
    return centred * rstd, rstd


def ln_rows(v, gain, bias):
    return ln_stats(v)[0] * gain + bias


def ln_back(v, gain, dh):
    hat, rstd = ln_stats(v)
    g = dh * gain
    dv = rstd * (
        g - jnp.mean(g, -1, keepdims=True) - hat * jnp.mean(g * hat, -1, keepdims=True)
    )
    return dv, dh * hat


def gelu_pair(z):
    size = jnp.abs(z)
    bell = jnp.exp(-0.5 * z * z)
    u = 1.0 / (1.0 + (0.3275911 * SQRT_HALF) * size)
    poly = u * (
        0.254829592
        + u * (-0.284496736 + u * (1.421413741 + u * (-1.453152027 + u * 1.061405429)))
    )
    tail = 0.5 * poly * bell
    below = jnp.where(z < 0.0, tail, 1.0 - tail)
    return below, z * bell * INV_SQRT_2PI


def by_heads(values, factor):
    lane = lax.broadcasted_iota(jnp.int32, (1, 2 * HEAD_DIM), 1)
    first = (lane < HEAD_DIM).astype(F32)
    return jnp.concatenate(
        [values * (first * factor).astype(BF), values * ((1.0 - first) * factor).astype(BF)], 0
    )


def softmax_rows(s, keep):
    if keep is not None:
        s = jnp.where(keep, s, NEG)
    ex = jnp.exp(s - jnp.max(s, 0, keepdims=True))
    return ex * (1.0 / jnp.sum(ex, 0, keepdims=True))


def by_head_lanes(both, factor=None):
    n = both.shape[0] // 2
    first = lax.broadcasted_iota(jnp.int32, (1, 2 * HEAD_DIM), 1) < HEAD_DIM
    out = jnp.where(first, both[:n], both[n:])
    return (out if factor is None else out * factor).astype(BF)


def attn_forward(qs, ks, vs, keep):
    scores = [nt(k, by_heads(q, SCALE)) for q, k in zip(qs, ks)]
    probs = [softmax_rows(s, keep).astype(BF) for s in scores]
    return [by_head_lanes(tn(p, v)) for p, v in zip(probs, vs)]


def attn_backward(qs, ks, vs, gs, keep):
    qms, gms = [by_heads(q, SCALE) for q in qs], [by_heads(g, 1.0) for g in gs]
    scores = [nt(k, qm) for k, qm in zip(ks, qms)]
    dps = [nt(v, gm) for v, gm in zip(vs, gms)]
    probs = [softmax_rows(s, keep) for s in scores]
    dss = [
        (p * (dp - jnp.sum(p * dp, 0, keepdims=True))).astype(BF) for p, dp in zip(probs, dps)
    ]
    lows = [p.astype(BF) for p in probs]
    dqs = [by_head_lanes(tn(ds, k), SCALE) for ds, k in zip(dss, ks)]
    dks = [nn(ds, qm).astype(BF) for ds, qm in zip(dss, qms)]
    dvs = [nn(p, gm).astype(BF) for p, gm in zip(lows, gms)]
    return dqs, dks, dvs


def head_lanes(first, count):
    return [slice(128 * j, 128 * (j + 1)) for j in range(first, first + count)]


def same_patch(rows, keys, group):
    a = lax.broadcasted_iota(jnp.int32, (rows, keys), 0)
    b = lax.broadcasted_iota(jnp.int32, (rows, keys), 1)
    return lax.rem(a, group) == lax.rem(b, group)


def remote(src, dst, send_sem, recv_sem, device):
    return pltpu.make_async_remote_copy(
        src_ref=src,
        dst_ref=dst,
        send_sem=send_sem,
        recv_sem=recv_sem,
        device_id=device,
        device_id_type=MESH_ID,
    )


def places():
    d, z, t = lax.axis_index("dp"), lax.axis_index("seq"), lax.axis_index("tensor")
    y, x = lax.div(d, 2), lax.rem(d, 2)
    across_x = (2 * y + 1 - x, z, t)
    across_y = (2 * (1 - y) + x, z, t)
    other = (d, z, 1 - t)
    along = [(d, lax.rem(z + j, NZ), t) for j in range(1, NZ)]
    return d, y, x, z, t, across_x, across_y, other, along


def add(total, part):
    total[...] = total[...] + part[...]


def greet(devices):
    barrier = pltpu.get_barrier_semaphore()
    for device in devices:
        pl.semaphore_signal(barrier, inc=1, device_id=device, device_id_type=MESH_ID)
    pl.semaphore_wait(barrier, len(devices))


NZ = 4
LINES = 96


def wide(pair):
    return jnp.concatenate([flat(pair[0]), flat(pair[1])], 1)


def lines(ref, i):
    per = ref.shape[1] // LINES
    if per == 1:
        return (i, slice(None), slice(None))
    start = pl.multiple_of(lax.rem(i, per) * LINES, LINES)
    return (lax.div(i, per), pl.ds(start, LINES), slice(None))


def forward_kernel(
    clips,
    cot,
    qkvw,
    outw,
    ffnw,
    norm,
    counts,
    wa_o,
    xt_o,
    h0_o,
    qkv0_o,
    os_o,
    y1_o,
    h1_o,
    qkv1_o,
    o1_o,
    dy2_o,
    lo_o,
    gf_o,
    block_o,
    ng_o,
    w,
    xt,
    xs,
    h0,
    qkv0,
    ot,
    os_,
    y1,
    h1,
    qkv1,
    o1,
    h3,
    ct,
    h3a,
    ea,
    h3t,
    et,
    acc,
    dh3,
    act,
    dz,
    wf,
    r1,
    r2,
    z1s,
    z1r,
    z2s,
    z3s,
    zpr,
    x1s,
    x1r,
    x2s,
    x2r,
    ks,
    kr,
    ts,
    tr,
    tl,
    es,
    er,
    el,
    sv,
    fs,
    fv,
    g2s,
    g2r,
    g3s,
    g3r,
):
    d, y, x, z, t, across_x, across_y, other, along = places()
    greet([across_x, across_y, other] + along)

    fr = clips.shape[1]
    half = clips.shape[2] // 2
    frames = NZ * fr
    fh = frames // 2
    mine = pl.ds(pl.multiple_of(t * half, half), half)

    def tokens_in(src, dst, which):
        here = dst.at[pl.ds(z * fr, fr)]
        own = pltpu.make_async_copy(src.at[z, :, mine], here, tl.at[which])
        own.start()
        copies = []
        for j, device in enumerate(along):
            copy = remote(
                src.at[device[1], :, mine], here, ts.at[which, j], tr.at[which, j], device
            )
            copy.start()
            copies.append(copy)
        return own, copies

    def tokens_wait(started):
        started[0].wait()
        for copy in started[1]:
            copy.wait_recv()

    def to_frames_half(src, dst, which):
        own = pltpu.make_async_copy(src.at[pl.ds(t * fh, fh)], dst.at[:, mine], el.at[which])
        own.start()
        copy = remote(
            src.at[pl.ds((1 - t) * fh, fh)], dst.at[:, mine], es.at[which], er.at[which], other
        )
        copy.start()
        return own, copy

    def exchange_wait(started):
        started[0].wait()
        started[1].wait_recv()

    pending = []

    def save(src, dst):
        copy = pltpu.make_async_copy(src, dst, sv.at[len(pending)])
        copy.start()
        pending.append(copy)
        return copy

    for i in range(2):
        for s in range(3):
            w[4 * i + s, t, y, x, z] = qkvw[i, s].astype(BF)
        w[4 * i + 3, t, y, x, z] = outw[i].astype(BF)
        for c in range(4):
            wf[2 * c + i, y, x, z] = ffnw[i, :, 384 * c : 384 * (c + 1)].astype(BF)

    inner = jnp.logical_or(z == 1, z == 2)
    near, far = 2 * lax.div(z, 2), 2 - 2 * lax.div(z, 2)
    partner, over = (d, z + 1 - 2 * lax.rem(z, 2), t), (d, NZ - 1 - z, t)

    def own(u):
        return w.at[u, t] if u < 8 else wf.at[u - 8]

    def z_one(u):
        ref = own(u).at[y, x, z]
        return remote(ref, ref, z1s.at[u], z1r.at[u], partner)

    def z_two(u):
        ref = own(u).at[y, x, pl.ds(near, 2)]
        return remote(ref, ref, z2s.at[u], zpr.at[u], over)

    def z_three(u):
        ref = own(u).at[y, x, pl.ds(far, 2)]
        return remote(ref, ref, z3s.at[u], zpr.at[u], partner)

    def plane_one(u, i):
        ref = own(u).at[y, x]
        return remote(ref, ref, x1s.at[u], x1r.at[u], across_y if i else across_x)

    def plane_two(u, i):
        ref = own(u).at[:, x] if i else own(u).at[y]
        return remote(ref, ref, x2s.at[u], x2r.at[u], across_x if i else across_y)

    def to_core(u):
        ref = w.at[u, t]
        return remote(ref, ref, ks.at[u], kr.at[u], other)

    def send_z1(p):
        for u in (2 * p, 2 * p + 1):
            z_one(u).start()

    def send_z2(p):
        for u in (2 * p, 2 * p + 1):
            z_one(u).wait_recv()

        @pl.when(inner)
        def _():
            for u in (2 * p, 2 * p + 1):
                z_two(u).start()

    def send_z3(p):
        @pl.when(inner)
        def _():
            for u in (2 * p, 2 * p + 1):
                z_three(u).wait_recv()
                z_three(u).start()

    def send_one(p):
        @pl.when(jnp.logical_not(inner))
        def _():
            for u in (2 * p, 2 * p + 1):
                z_three(u).wait_recv()

        for i in range(2):
            plane_one(2 * p + i, i).start()

    def send_two(p):
        for i in range(2):
            plane_one(2 * p + i, i).wait_recv()
            plane_two(2 * p + i, i).start()

    def send_core(p):
        for i in range(2):
            plane_two(2 * p + i, i).wait_recv()
            to_core(2 * p + i).start()

    def need(p):
        for i in range(2):
            u = 2 * p + i
            if u < 8:
                to_core(u).wait_recv()
                to_core(u).wait_send()
            else:
                plane_two(u, i).wait_recv()
            plane_one(u, i).wait_send()
            plane_two(u, i).wait_send()
            z_one(u).wait_send()

        @pl.when(inner)
        def _():
            for u in (2 * p, 2 * p + 1):
                z_two(u).wait_send()
                z_three(u).wait_send()

    def run(*events):
        for stage, p in events:
            stage(p)

    def at_step(i, k, *events):
        @pl.when(i == k)
        def _():
            run(*events)

    for stage in (send_z1, send_z2):
        for p in range(4):
            stage(p)
    run((send_z3, 0), (send_z3, 1))
    x_in = tokens_in(clips, xt, 0)
    run((send_z3, 2), (send_z3, 3), (send_one, 0), (send_one, 1))
    for p in range(4, 8):
        send_z1(p)
    run((send_one, 2), (send_two, 0), (send_two, 1), (send_core, 0), (send_one, 3))
    run((send_two, 2), (send_core, 1))
    need(0)
    need(1)

    gain, bias = norm[0:1, :], norm[3:4, :]

    def tokens_part(k, carry):
        base = lax.rem(z - k + NZ, NZ) * fr

        @pl.when(k == 0)
        def _():
            x_in[0].wait()

        @pl.when(k > 0)
        def _():
            j = jnp.maximum(k - 1, 0)
            here = xt.at[pl.ds(0, fr)]
            remote(here, here, ts.at[0, j], tr.at[0, j], other).wait_recv()

        for f in range(fr):
            h0[base + f] = ln_rows(xt[base + f].astype(F32), gain, bias).astype(BF)
        left = flat(h0[pl.ds(base, fr)])
        for s in range(3):
            part = nn(left, wide(w.at[s])).astype(BF)
            qkv0[s, pl.ds(base, fr)] = part.reshape((fr,) + h0.shape[1:])
        at_step(k, 0, (send_z2, 4), (send_z2, 5))
        at_step(k, 2, (send_z2, 6), (send_z2, 7), (send_z3, 4), (send_z3, 5))
        return carry

    lax.fori_loop(0, NZ, tokens_part, 0)
    x_ex = to_frames_half(xt, xs, 0)
    save(xt, xt_o)
    save(h0, h0_o)
    save(qkv0, qkv0_o)
    run((send_two, 3), (send_one, 4), (send_core, 2))

    def project(src, dst, u, s):
        lead = src.shape[0] // 2

        def block(i, carry):
            rows = pl.ds(i * lead, lead)
            part = nn(flat(src[rows]), wide(w.at[u])).astype(BF)
            dst[s, rows] = part.reshape((lead,) + src.shape[1:])
            return carry

        lax.fori_loop(0, 2, block, 0)

    keep = same_patch(frames * 16, 2 * frames * 16, 16)

    def temporal(b, carry):
        rows = pl.ds(pl.multiple_of(b * 16, 16), 16)
        for j in range(0, 6, 3):
            group = head_lanes(j, 3)
            parts = [[flat(qkv0[s, :, rows, at]) for at in group] for s in range(3)]
            for at, out in zip(group, attn_forward(*parts, keep)):
                ot[:, rows, at] = out.reshape((frames, 16, 128))
        at_step(b, 1, (send_z3, 6), (send_z3, 7))
        at_step(b, 3, (send_one, 5), (send_core, 3))
        at_step(b, 5, (send_two, 4))
        return carry

    lax.fori_loop(0, half // 16, temporal, 0)
    c_in = tokens_in(cot, ct, 1)
    o_ex = to_frames_half(ot, os_, 1)

    exchange_wait(x_ex)
    exchange_wait(o_ex)
    mixed_saved = save(os_, os_o)
    gain1, bias1 = norm[1:2, :], norm[4:5, :]

    def branch_sum(mixed, base, total, u, normed, gain, bias):
        def block(i, carry):
            two_frames = pl.ds(2 * i, 2)
            part = nt(flat(mixed[two_frames]), wide(w.at[u]))
            total[two_frames] = base[two_frames].astype(F32) + part.reshape(
                (2,) + mixed.shape[1:]
            )
            return carry

        lax.fori_loop(0, fh // 2, block, 0)

        def rescale(i, carry):
            at = lines(total, i)
            normed[at] = ln_rows(total[at], gain, bias).astype(BF)
            return carry

        lax.fori_loop(0, frames * half // LINES, rescale, 0, unroll=2)

    branch_sum(os_, xs, y1, 3, h1, gain1, bias1)
    y1_saved = save(y1, y1_o)
    h1_saved = save(h1, h1_o)
    run((send_one, 6), (send_two, 5))
    need(2)
    project(h1, qkv1, 4, 0)
    project(h1, qkv1, 5, 1)
    need(3)
    project(h1, qkv1, 6, 2)
    save(qkv1, qkv1_o)
    for u in range(8):
        save(w.at[u], wa_o.at[u])

    def spatial(b, carry):
        for j in range(0, 6, 2):
            group = head_lanes(j, 2)
            parts = [[qkv1[s, b, :, at] for at in group] for s in range(3)]
            for at, out in zip(group, attn_forward(*parts, None)):
                o1[b, :, at] = out
        at_step(b, 1, (send_one, 7))
        at_step(b, 3, (send_two, 6))
        return carry

    lax.fori_loop(0, fh, spatial, 0)
    save(o1, o1_o)
    gain2, bias2 = norm[2:3, :], norm[5:6, :]

    y1_saved.wait()
    branch_sum(o1, y1, y1, 7, h3, gain2, bias2)
    ours, others = pl.ds(t * fh, fh), pl.ds((1 - t) * fh, fh)

    def to_other(src, dst, which):
        copy = remote(src, dst, fs.at[which], fv.at[which], other)
        copy.start()
        return copy

    mixed_saved.wait()
    h3_ex = to_other(h3, h3a.at[ours], 0)
    h3_own = pltpu.make_async_copy(h3, h3a.at[ours], el.at[2])
    h3_own.start()
    tokens_wait(c_in)
    c_ex = to_other(ct, ea.at[:, mine], 1)
    c_own = pltpu.make_async_copy(ct, ea.at[:, mine], el.at[3])
    c_own.start()
    run((send_two, 7),)
    acc[...] = jnp.zeros_like(acc)
    dh3[...] = jnp.zeros_like(dh3)
    h3_own.wait()
    h3_ex.wait()

    def turn(src, dst):
        for i in range(2):
            block = slice(i * fh, (i + 1) * fh)
            lanes = slice(i * dst.shape[1] // 2, (i + 1) * dst.shape[1] // 2)
            dst[:, lanes] = flat(src[block]).T

    turn(h3a, h3t)
    c_own.wait()
    c_ex.wait()
    on = jnp.where(z < counts[0], 1.0, 0.0)

    def prepare(i, carry):
        ea[i] = (ea[i].astype(F32) * on).astype(BF)
        return carry

    lax.fori_loop(0, frames, prepare, 0)
    turn(ea, et)

    def give_one_copy(r):
        src = wf.at[r, :, 1 - x] if r % 2 else wf.at[r, 1 - y]
        return remote(src, r1.at[r], g2s.at[r], g2r.at[r], across_x if r % 2 else across_y)

    def give_two_copy(r):
        src = wf.at[r, 1 - y, x] if r % 2 else wf.at[r, y, 1 - x]
        return remote(src, r2.at[r], g3s.at[r], g3r.at[r], across_y if r % 2 else across_x)

    def give_one(r):
        give_one_copy(r).start()

    def give_two(r):
        give_one_copy(r).wait_recv()
        total, part = wf.at[r], r1.at[r]
        add(total.at[(1 - y, x) if r % 2 else (y, 1 - x)], part.at[1 - y if r % 2 else 1 - x])
        give_two_copy(r).start()
        add(total.at[y, x], part.at[y if r % 2 else x])

    def give_last(r):
        give_two_copy(r).wait_recv()
        block = wf.at[r, y, x]
        add(block, r2.at[r])
        save(block, block_o.at[r])

    def hidden_half(c, carry):
        for k in range(2):

            @pl.when(c == k)
            def _():
                need(4 + 2 * k)
                need(5 + 2 * k)

        def side(first):
            return jnp.concatenate([flat(wf[4 * c + first]), flat(wf[4 * c + first + 2])], 1)

        def some_tokens(i, carry):
            f0, f1 = side(0), side(1)
            here = pl.ds(2 * i, 2)
            rows = pl.ds(pl.multiple_of(i * 4 * half, 4 * half), 4 * half)
            pre = nn(flat(h3a[here]), f0)
            below, slope = gelu_pair(pre)
            active = (pre * below).astype(BF)
            act[rows, :] = active
            back = (nn(flat(ea[here]), f1) * (below + slope)).astype(BF)
            dz[rows, :] = back
            shape = (2,) + ea.shape[1:]
            acc[here] += nt(active, f1).reshape(shape)
            dh3[here] += nt(back, f0).reshape(shape)
            return carry

        lax.fori_loop(0, frames // 2, some_tokens, 0)
        for first, left, right in ((0, h3t, dz), (1, et, act)):

            def some_rows(i, carry):
                rows = pl.ds(pl.multiple_of(i * 384, 384), 384)
                total = nn(left[rows, :], right[...]).astype(BF)
                for k in range(2):
                    part = total[:, 384 * k : 384 * (k + 1)]
                    wf[4 * c + first + 2 * k, i] = part.reshape(wf.shape[2:])
                return carry

            lax.fori_loop(0, 2, some_rows, 0)
        at_step(c, 0, *[(give_one, r) for r in range(4)])
        return carry

    lax.fori_loop(0, 2, hidden_half, 0)
    save(wf.at[pl.ds(4, 4)], gf_o)
    for i in range(fh):
        h3a[(1 - t) * fh + i] = acc[(1 - t) * fh + i].astype(BF)
    out_ex = to_other(h3a.at[others], xs, 2)
    for i in range(fh):
        ea[(1 - t) * fh + i] = dh3[(1 - t) * fh + i].astype(BF)
    dh_ex = to_other(ea.at[others], os_, 3)
    for r in range(4):
        give_two(r)

    def finish(i, sums):
        at = lines(y1, i)
        here = (t * fh + at[0],) + at[1:]
        v = y1[at]
        up = dh3[here] + os_[at].astype(F32)
        h1[at] = (v + (acc[here] + xs[at].astype(F32))).astype(BF)
        dv, dg = ln_back(v, gain2, up)
        dh3[here] = ea[here].astype(F32) + dv
        return (
            sums[0] + jnp.sum(dg, 0, keepdims=True),
            sums[1] + jnp.sum(up, 0, keepdims=True),
        )

    h1_saved.wait()
    out_ex.wait()
    dh_ex.wait()
    zero = jnp.zeros((1, norm.shape[1]), F32)
    dg, db = lax.fori_loop(0, frames * half // LINES, finish, (zero, zero), unroll=2)
    ng_o[...] = jnp.zeros_like(ng_o)
    ng_o[2:3, :] = dg
    ng_o[5:6, :] = db
    save(h1, lo_o)
    save(dh3.at[ours], dy2_o)
    for r in range(4):
        give_last(r)
    for r in range(4):
        give_one_copy(r).wait_send()
        give_two_copy(r).wait_send()
    for started in (x_in, c_in):
        for copy in started[1]:
            copy.wait_send()
    for started in (x_ex, o_ex):
        started[1].wait_send()
    for copy in pending:
        if all(copy is not early for early in (mixed_saved, y1_saved, h1_saved)):
            copy.wait()


RS_ORDER = [8, 9, 10, 11, 12, 13, 14, 15, 7, 4, 5, 6, 3, 0, 1, 2]
GROUPS = [[0, 1], [2, 3], [4, 5], [6, 7], [8], [9, 10], [11, 12], [13, 14], [15]]


def backward_kernel(
    wa_i,
    xt_i,
    h0_i,
    qkv0_i,
    os_i,
    y1_i,
    h1_i,
    qkv1_i,
    o1_i,
    dy2_i,
    lo_i,
    gf_i,
    block_i,
    norm,
    ng_i,
    qkv_row,
    out_row,
    ffn_row,
    gsum,
    row_o,
    pack_o,
    lo_t,
    lo_o,
    gi_o,
    wa,
    xt,
    h0,
    qkv0,
    os_,
    y1,
    h1,
    qkv1,
    o1,
    dy,
    e,
    et,
    ht,
    do,
    e0,
    gt,
    dh,
    pf,
    block,
    tg,
    gr,
    r1,
    r2,
    r3,
    ld,
    pd,
    ks,
    kr,
    x1s,
    x1r,
    x2s,
    x2r,
    z1s,
    z1r,
    z2s,
    z2r,
    z3s,
    z3r,
    es,
    er,
    el,
    ts,
    tr,
    tl,
    ss,
    sr,
    as_,
    ar,
    row_in,
    pack_in,
    held,
):
    d, y, x, z, t, across_x, across_y, other, along = places()
    greet([across_x, across_y, (3 - d, z, t), other] + along)

    half = xt.shape[1]
    frames = xt.shape[0]
    fh = frames // 2
    fr = frames // NZ
    mine = pl.ds(pl.multiple_of(t * half, half), half)
    theirs = pl.ds(pl.multiple_of((1 - t) * half, half), half)

    loads = {}

    def load(name, src, dst):
        loads[name] = pltpu.make_async_copy(src, dst, ld.at[len(loads)])
        loads[name].start()

    def own_part(r):
        return pltpu.make_async_copy(gf_i.at[r - 4], pf.at[r - 4], pd.at[r])

    def block_in(r):
        return pltpu.make_async_copy(block_i.at[r], block.at[r], pd.at[r])

    def halves(r):
        return tg.at[r - 13] if r >= 13 else wa.at[RS_ORDER[r]]

    def grad_ref(r):
        return pf.at[r - 4] if r < 8 else halves(r).at[t]

    def block_ref(r):
        return block.at[r] if r < 4 else grad_ref(r).at[y, x]

    inner = jnp.logical_or(z == 1, z == 2)
    near, far = 2 * lax.div(z, 2), 2 - 2 * lax.div(z, 2)
    pair = z + 1 - 2 * lax.rem(z, 2)
    partner, over = (d, pair, t), (d, NZ - 1 - z, t)

    def core_copy(r):
        return remote(halves(r).at[1 - t], gr.at[r - 8], ks.at[r], kr.at[r], other)

    def one_copy(r):
        total = grad_ref(r)
        src = total.at[:, 1 - x] if r % 2 else total.at[1 - y]
        device = across_x if r % 2 else across_y
        return remote(src, r1.at[r - 4], x1s.at[r], x1r.at[r], device)

    def two_copy(r):
        total = grad_ref(r)
        src = total.at[1 - y, x] if r % 2 else total.at[y, 1 - x]
        device = across_y if r % 2 else across_x
        return remote(src, r2.at[r - 4], x2s.at[r], x2r.at[r], device)

    def send_core(rs):
        for r in rs:
            core_copy(r).start()

    def send_one(rs):
        for r in rs:
            if r < 8:
                own_part(r).wait()
                one_copy(r).start()
                continue
            core_copy(r).wait_recv()
            total, part = grad_ref(r), gr.at[r - 8]
            away = [(i, 1 - x) if r % 2 else (1 - y, i) for i in range(2)]
            keep = [(i, x) if r % 2 else (y, i) for i in range(2)]
            for at in away:
                add(total.at[at], part.at[at])
            one_copy(r).start()
            for at in keep:
                add(total.at[at], part.at[at])

    def send_two(rs):
        for r in rs:
            one_copy(r).wait_recv()
            total, part = grad_ref(r), r1.at[r - 4]
            add(total.at[(1 - y, x) if r % 2 else (y, 1 - x)], part.at[1 - y if r % 2 else 1 - x])
            two_copy(r).start()
            add(total.at[y, x], part.at[y if r % 2 else x])

    def z_in(r):
        src = block_ref(r).at[pl.ds(far, 2)]
        return remote(src, r3.at[r, pl.ds(0, 2)], z1s.at[r], z1r.at[r], partner)

    def z_across(r):
        src = block_ref(r).at[pl.ds(far, 2)]
        return remote(src, r3.at[r, pl.ds(2, 2)], z2s.at[r], z2r.at[r], over)

    def z_pair(r):
        return remote(
            block_ref(r).at[pair], r3.at[r, 4], z3s.at[r], z3r.at[r], partner
        )

    def z_direct(r):
        sems = ((z1s, z1r), (z2s, z2r), (z3s, z3r))
        return [
            remote(block_ref(r).at[device[1]], r3.at[r, j], ss.at[r], rr.at[r], device)
            for j, (device, (ss, rr)) in enumerate(zip(along, sems))
        ]

    def send_in(rs):
        for r in rs:
            if r < 4:
                block_in(r).wait()
            else:
                two_copy(r).wait_recv()
                add(block_ref(r), r2.at[r - 4])

        for r in rs:
            if r >= 13:
                for copy in z_direct(r):
                    copy.start()
        if rs[0] < 13:

            @pl.when(jnp.logical_not(inner))
            def _():
                for r in rs:
                    z_in(r).start()

    def send_across(rs):
        @pl.when(inner)
        def _():
            for r in rs:
                z_in(r).wait_recv()
                add(block_ref(r).at[pl.ds(far, 2)], r3.at[r, pl.ds(0, 2)])
                z_across(r).start()

    def send_pair(rs):
        @pl.when(inner)
        def _():
            for r in rs:
                z_across(r).wait_recv()
                add(block_ref(r).at[pl.ds(near, 2)], r3.at[r, pl.ds(2, 2)])

        for r in rs:
            z_pair(r).start()

    lane = lax.broadcasted_iota(jnp.int32, row_o.shape, 1)
    row_o[...] = jnp.zeros_like(row_o)
    pack_o[...] = jnp.zeros_like(pack_o)

    def settle(rs):
        for r in rs:
            u = RS_ORDER[r]
            total = block_ref(r)[z].astype(F32)
            if r < 13:
                z_pair(r).wait_recv()
                total += r3[r, 4].astype(F32)
            else:
                for j, copy in enumerate(z_direct(r)):
                    copy.wait_recv()
                    total += r3[r, j].astype(F32)
            gsum[u] = total
            square = total * total + EPS_ONE
            m = [k for k in range(10) if u in UNIT_OF[k]][0]
            row_o[...] += jnp.where(lane == m, jnp.sum(square, -1, keepdims=True), 0.0)
            pack_o[u : u + 1, :] = jnp.sum(square, 0, keepdims=True)

    def run(*events):
        for stage, k in events:
            stage(GROUPS[k])

    load("dy", dy2_i, dy)
    for r in range(4):
        block_in(r).start()
    for r in range(4, 8):
        own_part(r).start()
    load("o1", o1_i, o1)
    load("w1", wa_i.at[pl.ds(4, 4)], wa.at[pl.ds(4, 4)])
    load("qkv1", qkv1_i, qkv1)
    load("h1", h1_i, h1)
    load("y1", y1_i, y1)

    def to_patch_half(src, dst, which):
        own = pltpu.make_async_copy(src.at[:, mine], dst.at[pl.ds(t * fh, fh)], el.at[which])
        own.start()
        copy = remote(
            src.at[:, theirs], dst.at[pl.ds(t * fh, fh)], es.at[which], er.at[which], other
        )
        copy.start()
        return own, copy

    def exchange_wait(started):
        started[0].wait()
        started[1].wait_recv()

    lo_ex = to_patch_half(lo_i, lo_t, 0)
    load("xt", xt_i, xt)
    load("h0", h0_i, h0)
    load("w0", wa_i.at[pl.ds(0, 4)], wa.at[pl.ds(0, 4)])
    load("os", os_i, os_)
    load("qkv0", qkv0_i, qkv0)

    def tokens_out(src, dst, which, start, count):
        span = pl.ds(start, count)
        there = pl.ds(pl.multiple_of(t * half + start, 16), count)
        own = pltpu.make_async_copy(
            src.at[pl.ds(z * fr, fr), span], dst.at[z, :, there], tl.at[which]
        )
        own.start()
        copies = []
        for j, device in enumerate(along):
            copy = remote(
                src.at[pl.ds(device[1] * fr, fr), span],
                dst.at[z, :, there],
                ts.at[which, j],
                tr.at[which, j],
                device,
            )
            copy.start()
            copies.append(copy)
        return own, copies

    def share(dst, several, which, start, count):
        for started in several:
            started[0].wait()
            for copy in started[1]:
                copy.wait_recv()
        at = dst.at[:, :, pl.ds(pl.multiple_of(t * half + start, 16), count)]
        copy = remote(at, at, ss.at[which], sr.at[which], other)
        copy.start()
        return copy

    def transposed(src, dst):
        lead = src.shape[0] // 2
        for i in range(2):
            dst[:, 384 * i : 384 * (i + 1)] = flat(src[lead * i : lead * (i + 1)]).T

    def put_grad(dst, left, right):
        def block(i, carry):
            rows = pl.ds(pl.multiple_of(i * 384, 384), 384)
            total = nn(left[rows, :], right()).astype(BF)
            for h in range(2):
                dst[h, i] = total[:, 384 * h : 384 * (h + 1)].reshape(wa.shape[3:])
            return carry

        lax.fori_loop(0, 2, block, 0)

    def out_back(e_ref, u):
        lead = e_ref.shape[0] // 2

        def block(i, carry):
            left = flat(e_ref[pl.ds(i * lead, lead)])
            part = nn(left, wide(wa.at[u])).astype(BF)
            do[pl.ds(i * fh, fh)] = part.reshape((fh,) + do.shape[1:])
            return carry

        lax.fori_loop(0, 2, block, 0)

    zero = jnp.zeros((1, norm.shape[1]), F32)

    def norm_branch(stack, block, u, values, run, gain, put, carry):
        total = None
        for s in range(3):
            part = nt(flat(stack[(s,) + block]), wide(wa.at[u + s]))
            total = part if total is None else total + part
        dh[...] = total

        def line(k, sums):
            at = run(k)
            up = dh[pl.ds(pl.multiple_of(k * LINES, LINES), LINES), :]
            dv, dg = ln_back(flat(values[at]).astype(F32), gain, up)
            put(at, dv)
            return (
                sums[0] + jnp.sum(dg, 0, keepdims=True),
                sums[1] + jnp.sum(up, 0, keepdims=True),
            )

        return lax.fori_loop(0, dh.shape[0] // LINES, line, carry, unroll=2)

    loads["dy"].wait()

    def low_one(i, carry):
        e[i] = dy[i].astype(BF)
        return carry

    lax.fori_loop(0, fh, low_one, 0)
    run((send_one, 2), (send_in, 0), (send_in, 1), (send_one, 3))
    loads["o1"].wait()
    loads["w1"].wait()
    out_back(e, 7)
    transposed(e, et)
    put_grad(wa.at[7], et, lambda: flat(o1[...]))
    run((send_core, 4), (send_across, 0), (send_across, 1))
    loads["qkv1"].wait()

    def spatial(b, carry):
        for s in range(3):
            held[s] = qkv1[s, b]
        held[3] = flat(do[pl.ds(2 * b, 2)])
        for j in range(0, 6, 2):
            group = head_lanes(j, 2)
            parts = [[held[s, :, at] for at in group] for s in range(4)]
            for s, outs in enumerate(attn_backward(*parts, None)):
                for at, out in zip(group, outs):
                    qkv1[s, b, :, at] = out

        @pl.when(b == 0)
        def _():
            run((send_pair, 0), (send_pair, 1), (send_one, 4))

        @pl.when(b == 1)
        def _():
            run((send_two, 2), (settle, 0), (settle, 1))

        @pl.when(b == 2)
        def _():
            run((send_two, 3), (send_in, 2))

        @pl.when(b == 3)
        def _():
            run((send_two, 4), (send_across, 2))

        return carry

    lax.fori_loop(0, fh, spatial, 0)
    loads["h1"].wait()
    loads["y1"].wait()

    def put_two(at, dv):
        total = dy[at] + dv
        dy[at] = total
        e[at] = total.astype(BF)

    def spatial_block(i, carry):
        return norm_branch(
            qkv1,
            (pl.ds(i * fh // 2, fh // 2),),
            4,
            y1,
            lambda k: lines(y1, i * fh + k),
            norm[1:2, :],
            put_two,
            carry,
        )

    dg1, db1 = lax.fori_loop(0, 2, spatial_block, (zero, zero))
    e_ex = to_patch_half(e, e0, 1)
    exchange_wait(lo_ex)
    lo_out = [tokens_out(lo_t, lo_o, 0, 0, half)]
    run((send_in, 3), (send_pair, 2))
    transposed(h1, ht)
    put_grad(wa.at[4], ht, lambda: flat(qkv1[0]))
    put_grad(wa.at[5], ht, lambda: flat(qkv1[1]))
    run((send_core, 5), (send_in, 4), (send_across, 3))
    put_grad(wa.at[6], ht, lambda: flat(qkv1[2]))

    transposed(e, et)
    loads["w0"].wait()
    loads["os"].wait()
    exchange_wait(e_ex)
    out_back(e0, 3)
    put_grad(wa.at[3], et, lambda: flat(os_[...]))
    run((send_core, 6), (send_one, 5), (send_across, 4), (send_pair, 3), (settle, 2))
    loads["qkv0"].wait()
    keep = same_patch(frames * 16, 2 * frames * 16, 16)

    def temporal(b, carry):
        rows = pl.ds(pl.multiple_of(b * 16, 16), 16)
        n = frames * 16
        for s in range(3):
            held[s, 0:n] = flat(qkv0[s, :, rows])
        held[3, 0:n] = flat(do[:, rows])
        for j in range(0, 6, 3):
            group = head_lanes(j, 3)
            parts = [[held[s, 0:n, at] for at in group] for s in range(4)]
            for s, outs in enumerate(attn_backward(*parts, keep)):
                for at, out in zip(group, outs):
                    qkv0[s, :, rows, at] = out.reshape((frames, 16, 128))
        return carry

    def put_one(at, dv):
        total = flat(e0[at]).astype(F32) + dv
        gt[at] = total.astype(BF).reshape((2, half // 2, dv.shape[1]))

    def temporal_norm(i, sums):
        span = slice(i * half // 2, (i + 1) * half // 2)
        return norm_branch(
            qkv0,
            (slice(None), span),
            0,
            xt,
            lambda k: (pl.ds(2 * k, 2), span),
            norm[0:1, :],
            put_one,
            sums,
        )

    loads["xt"].wait()
    lax.fori_loop(0, half // 32, temporal, 0)
    run((send_one, 6), (send_two, 5), (send_pair, 4), (settle, 3))
    sums = temporal_norm(0, (zero, zero))
    gi_out = [tokens_out(gt, gi_o, 1, 0, half // 2)]
    run((send_two, 6), (send_in, 5), (settle, 4))
    loads["h0"].wait()
    transposed(h0, ht)
    lax.fori_loop(half // 32, half // 16, temporal, 0)
    run((send_in, 6), (send_across, 5))
    put_grad(tg.at[0], ht, lambda: flat(qkv0[0]))
    put_grad(tg.at[1], ht, lambda: flat(qkv0[1]))
    run((send_core, 7),)
    put_grad(tg.at[2], ht, lambda: flat(qkv0[2]))
    run((send_core, 8), (send_one, 7), (send_across, 6), (send_pair, 5))
    sums = temporal_norm(1, sums)
    gi_out.append(tokens_out(gt, gi_o, 2, half // 2, half // 2))
    run((send_one, 8), (send_two, 7), (send_pair, 6), (settle, 5))
    norm_rows = jnp.concatenate(
        [sums[0], dg1, ng_i[2:3, :], sums[1], db1, ng_i[5:6, :], jnp.zeros((2, dg1.shape[1]), F32)],
        0,
    )
    pack_o[16:24, :] = norm_rows[:, :384]
    pack_o[24:32, :] = norm_rows[:, 384:]
    run((send_two, 8), (send_in, 7), (settle, 6), (send_in, 8), (settle, 7))
    run((settle, 8),)

    first = remote(row_o, row_in, as_.at[0], ar.at[0], other)
    first.start()
    part = pl.ds(16, 16)
    second = remote(pack_o.at[part], pack_in.at[0, part], as_.at[1], ar.at[1], other)
    second.start()
    lo_share = share(lo_o, lo_out, 0, 0, half)
    gi_share = [share(gi_o, gi_out[:1], 1, 0, half // 2)]
    first.wait()
    second.wait()
    row_o[...] = row_o[...] + row_in[...]
    pack_o[16:32, :] = pack_o[16:32, :] + pack_in[0, 16:32, :]
    pack_o[32:33, 0:128] = jnp.sum(row_o[...], 0, keepdims=True)
    old = jnp.zeros((1, 128), F32)
    mats = [(qkv_row[m // 3], m % 3) for m in range(6)]
    mats += [(ref[...], k) for ref in (out_row, ffn_row) for k in range(2)]
    for m, (values, k) in enumerate(mats):
        old = jnp.where(lane[0:1] == m, jnp.sum(values[k : k + 1], -1, keepdims=True), old)
    pack_o[32:33, 128:256] = old
    for base, devices in ((1, (across_x, across_y, (3 - d, z, t))), (4, along)):
        copies = []
        for k, device in enumerate(devices):
            copy = remote(
                pack_o, pack_in.at[base + k], as_.at[1 + base + k], ar.at[1 + base + k], device
            )
            copy.start()
            copies.append(copy)
        if base == 4:
            gi_share.append(share(gi_o, gi_out[1:], 2, half // 2, half // 2))
        for copy in copies:
            copy.wait()
        pack_o[...] = (pack_o[...] + pack_in[base]) + (pack_in[base + 1] + pack_in[base + 2])

    for r in range(16):
        if r >= 8:
            core_copy(r).wait_send()
        if r >= 4:
            one_copy(r).wait_send()
            two_copy(r).wait_send()
        for copy in [z_pair(r)] if r < 13 else z_direct(r):
            copy.wait_send()

    @pl.when(inner)
    def _():
        for r in range(13):
            z_across(r).wait_send()

    @pl.when(jnp.logical_not(inner))
    def _():
        for r in range(13):
            z_in(r).wait_send()

    for copy in (lo_ex[1], e_ex[1]):
        copy.wait_send()
    for started in lo_out + gi_out:
        for copy in started[1]:
            copy.wait_send()
    for copy in [lo_share] + gi_share:
        copy.wait_send()
        copy.wait_recv()


UNIT_OF = [(0,), (1,), (2,), (4,), (5,), (6,), (3,), (7,), (8, 10, 12, 14), (9, 11, 13, 15)]


def update_kernel(
    gsum,
    row_sum,
    pack,
    qkv_row,
    out_row,
    ffn_row,
    qkv_col,
    out_col,
    ffn_col,
    qkvw,
    outw,
    ffnw,
    norm,
    moment,
    lo,
    gi,
    lo_o,
    gi_o,
    norm_g,
    norm_m,
    norm_n,
    qkv_g,
    qkv_n,
    out_g,
    out_n,
    ffn_g,
    ffn_n,
    qkv_r,
    out_r,
    ffn_r,
    qkv_c,
    out_c,
    ffn_c,
    rows_s,
    cols_s,
    mean_s,
):
    step = pl.program_id(0)
    decay = 1.0 - STEP ** (-0.8)
    width = norm.shape[1]
    n = row_sum.shape[0]

    @pl.when(step == 0)
    def _():
        lane = lax.broadcasted_iota(jnp.int32, (1, 128), 1)
        across = jnp.where(lane < 8, 1.0 / width, 1.0 / (8 * 384))
        old = jnp.concatenate(
            [qkv_row[0], qkv_row[1], out_row[...], ffn_row[...], jnp.zeros((118, n), F32)], 0
        )
        row_new = decay * old.T + (1.0 - decay) * (row_sum[...] * across)
        rows_s[...] = row_new
        row_t = row_new.T
        mean_s[...] = decay * (pack[32:33, 128:256] * (1.0 / width)) + (1.0 - decay) * (
            pack[32:33, 0:128] * across * (1.0 / width)
        )

        def column(old_col, u):
            fresh = decay * old_col + (1.0 - decay) * (pack[u : u + 1, :] * (1.0 / width))
            cols_s[u : u + 1, :] = fresh
            return fresh

        for i in range(2):
            qkv_r[i] = row_t[3 * i : 3 * i + 3]
            for k in range(3):
                qkv_c[i, k : k + 1, :] = column(qkv_col[i, k : k + 1, :], 4 * i + k)
            out_c[i : i + 1, :] = column(out_col[i : i + 1, :], 4 * i + 3)
            for c in range(4):
                lanes = slice(384 * c, 384 * (c + 1))
                ffn_c[i : i + 1, lanes] = column(ffn_col[i : i + 1, lanes], 8 + 2 * c + i)
        out_r[...] = row_t[6:8]
        ffn_r[...] = row_t[8:10]
        grad = jnp.concatenate([pack[16:22, :], pack[24:30, :]], 1)
        norm_g[...] = grad
        fresh = decay * moment[...] + (1.0 - decay) * (grad * grad + EPS_ONE)
        norm_m[...] = fresh
        update = grad * lax.rsqrt(fresh)
        rms = jnp.sqrt(jnp.mean(update * update, -1, keepdims=True))
        norm_n[...] = norm[...] - RATE_NORM * (update / jnp.maximum(1.0, rms))

    lo_o[...] = lo[...]
    gi_o[...] = gi[...].astype(F32)

    def change(k, m, u, rate):
        second = (
            rows_s[:, m : m + 1] * cols_s[u : u + 1, :] / mean_s[:, m : m + 1]
        )
        return rate * (gsum[k] * lax.rsqrt(second))

    for i in range(2):

        @pl.when(step == i)
        def _():
            for k in range(3):
                qkv_g[0, k] = gsum[k]
                qkv_n[0, k] = qkvw[0, k] - change(k, 3 * i + k, 4 * i + k, RATE_QKV)
            out_g[0] = gsum[3]
            out_n[0] = outw[0] - change(3, 6 + i, 4 * i + 3, RATE_OUT)

        @pl.when(step == 2 + i)
        def _():
            for k in range(4):
                c, m = k // 2, k % 2
                lanes = slice(384 * c, 384 * (c + 1))
                ffn_g[m, :, lanes] = gsum[k]
                ffn_n[m, :, lanes] = ffnw[m, :, lanes] - change(
                    k, 8 + m, 8 + 4 * i + k, (0.02, 0.01)[m]
                )


def call(kernel, outs, in_spaces, scratch, limit, collective=None, out_spaces=None):
    extra = {}
    if collective is not None:
        extra = dict(collective_id=collective, has_side_effects=True)
    out_spaces = out_spaces or [pltpu.VMEM] * len(outs)
    return pl.pallas_call(
        kernel,
        out_shape=[jax.ShapeDtypeStruct(shape, kind) for shape, kind in outs],
        in_specs=[pl.BlockSpec(memory_space=space) for space in in_spaces],
        out_specs=[pl.BlockSpec(memory_space=space) for space in out_spaces],
        scratch_shapes=scratch,
        compiler_params=pltpu.CompilerParams(vmem_limit_bytes=limit, **extra),
    )


def per_device_kernels(
    clips,
    cotangent,
    clip_counts,
    norm_params,
    norm_moment,
    qkv_weight,
    qkv_row,
    qkv_col,
    out_weight,
    out_row,
    out_col,
    ffn_weight,
    ffn_row,
    ffn_col,
):
    slots, per, patches, width = clips.shape
    frames = per * NZ
    rows = qkv_weight.shape[2]
    half = patches // 2
    vm, hbm = pltpu.VMEM, pl.ANY
    dma = pltpu.SemaphoreType.DMA
    by_patch = (frames, half, width)
    by_frame = (frames // 2, patches, width)
    unit = (2, 2, NZ, rows, 384)
    saved = [
        ((8, 2) + unit, BF),
        (by_patch, BF),
        (by_patch, BF),
        ((3,) + by_patch, BF),
        (by_frame, BF),
        (by_frame, F32),
        (by_frame, BF),
        ((3,) + by_frame, BF),
        (by_frame, BF),
        (by_frame, F32),
        (by_frame, BF),
        ((4,) + unit, BF),
        ((4, NZ, rows, 384), BF),
        ((8, width), F32),
    ]
    tokens = by_frame[0] * by_frame[1]
    kept = call(
        forward_kernel,
        saved,
        [hbm, hbm, vm, vm, vm, vm, pltpu.SMEM],
        [
            vm((8, 2) + unit, BF),
            vm(by_patch, BF),
            vm(by_frame, BF),
            vm(by_patch, BF),
            vm((3,) + by_patch, BF),
            vm(by_patch, BF),
            vm(by_frame, BF),
            vm(by_frame, F32),
            vm(by_frame, BF),
            vm((3,) + by_frame, BF),
            vm(by_frame, BF),
            vm(by_frame, BF),
            vm(by_patch, BF),
            vm((frames, patches, width), BF),
            vm((frames, patches, width), BF),
            vm((width, 2 * tokens), BF),
            vm((width, 2 * tokens), BF),
            vm((frames, patches, width), F32),
            vm((frames, patches, width), F32),
            vm((2 * tokens, 768), BF),
            vm((2 * tokens, 768), BF),
            vm((8,) + unit, BF),
            vm((4, 2, NZ, rows, 384), BF),
            vm((4, NZ, rows, 384), BF),
        ]
        + [dma((16,))] * 11
        + [
            dma((2, 3)),
            dma((2, 3)),
            dma((2,)),
            dma((3,)),
            dma((3,)),
            dma((4,)),
            dma((40,)),
        ]
        + [dma((4,))] * 6,
        LIMIT,
        0,
        [hbm] * 13 + [vm],
    )(clips, cotangent, qkv_weight, out_weight, ffn_weight, norm_params, clip_counts)
    clip_half = (slots, per, patches, width)
    gsum, row_sum, pack, unused, layer_out, grad_low = call(
        backward_kernel,
        [
            ((16, rows, 384), F32),
            ((rows, 128), F32),
            ((40, 384), F32),
            (by_patch, BF),
            (clip_half, BF),
            (clip_half, BF),
        ],
        [hbm] * 13 + [vm] * 5,
        [
            vm((8, 2) + unit, BF),
            vm(by_patch, BF),
            vm(by_patch, BF),
            vm((3,) + by_patch, BF),
            vm(by_frame, BF),
            vm(by_frame, F32),
            vm(by_frame, BF),
            vm((3,) + by_frame, BF),
            vm(by_frame, BF),
            vm(by_frame, F32),
            vm(by_frame, BF),
            vm((width, tokens), BF),
            vm((width, tokens), BF),
            vm(by_patch, BF),
            vm(by_patch, BF),
            vm(by_patch, BF),
            vm((tokens // 2, width), F32),
            vm((4,) + unit, BF),
            vm((4, NZ, rows, 384), BF),
            vm((3, 2) + unit, BF),
            vm((8,) + unit, BF),
            vm((12, 2, NZ, rows, 384), BF),
            vm((12, NZ, rows, 384), BF),
            vm((16, 5, rows, 384), BF),
            dma((12,)),
            dma((8,)),
        ]
        + [dma((16,))] * 12
        + [
            dma((2,)),
            dma((2,)),
            dma((2,)),
            dma((3, 3)),
            dma((3, 3)),
            dma((3,)),
            dma((3,)),
            dma((3,)),
            dma((8,)),
            dma((8,)),
            vm((rows, 128), F32),
            vm((7, 40, 384), F32),
            vm((4, patches, width), BF),
        ],
        LIMIT,
        1,
        [vm, vm, vm, hbm, hbm, hbm],
    )(*kept[:13], norm_params, kept[13], qkv_row, out_row, ffn_row)
    small = ((6, width), F32)
    shapes = [(a.shape, F32) for a in (qkv_weight, out_weight, ffn_weight)]
    states = (qkv_row, out_row, ffn_row, qkv_col, out_col, ffn_col)
    whole = pl.BlockSpec(memory_space=vm)
    clip = pl.BlockSpec((1,) + clip_half[1:], lambda c: (c, 0, 0, 0))
    four = pl.BlockSpec((4, rows, 384), lambda c: (c, 0, 0))
    one_qkv = pl.BlockSpec((1, 3, rows, 384), lambda c: (jnp.minimum(c, 1), 0, 0, 0))
    one_out = pl.BlockSpec((1, rows, 384), lambda c: (jnp.minimum(c, 1), 0, 0))
    half_ffn = pl.BlockSpec((2, rows, 768), lambda c: (0, 0, jnp.maximum(c - 2, 0)))
    weights = [one_qkv, one_out, half_ffn]
    outs = (
        [(clip_half, BF), (clip_half, F32)]
        + [small] * 3
        + [shapes[0]] * 2
        + [shapes[1]] * 2
        + [shapes[2]] * 2
        + [(a.shape, F32) for a in states]
    )
    results = pl.pallas_call(
        update_kernel,
        grid=(slots,),
        out_shape=[jax.ShapeDtypeStruct(shape, kind) for shape, kind in outs],
        in_specs=[four] + [whole] * 8 + weights + [whole] * 2 + [clip, clip],
        out_specs=[clip, clip]
        + [whole] * 3
        + [spec for spec in weights for k in range(2)]
        + [whole] * 6,
        scratch_shapes=[vm((rows, 128), F32), vm((16, 384), F32), vm((1, 128), F32)],
        compiler_params=pltpu.CompilerParams(vmem_limit_bytes=LIMIT),
    )(
        gsum,
        row_sum,
        pack,
        *states,
        qkv_weight,
        out_weight,
        ffn_weight,
        norm_params,
        norm_moment,
        layer_out,
        grad_low,
    )
    lo, gi, norm_g, norm_m, norm_n, *rest = results
    qkv_g, qkv_n, out_g, out_n, ffn_g, ffn_n, *moments = rest
    qkv_r, out_r, ffn_r, qkv_c, out_c, ffn_c = moments
    return (
        lo,
        gi,
        norm_g,
        norm_m,
        norm_n,
        qkv_g,
        qkv_n,
        qkv_r,
        qkv_c,
        out_g,
        out_n,
        out_r,
        out_c,
        ffn_g,
        ffn_n,
        ffn_r,
        ffn_c,
    )


LIMIT = 63 * 1024 * 1024


def solution(mesh):
    in_specs = (
        P("dp", "seq", None, None),
        P("dp", "seq", None, None),
        P("dp"),
        P(),
        P(),
        P(None, None, ("dp", "seq"), "tensor"),
        P(None, None, ("dp", "seq")),
        P(None, None, "tensor"),
        P(None, ("dp", "seq"), "tensor"),
        P(None, ("dp", "seq")),
        P(None, "tensor"),
        P(None, ("dp", "seq"), "tensor"),
        P(None, ("dp", "seq")),
        P(None, "tensor"),
    )
    out_specs = (
        P("dp", "seq", None, None),
        P("dp", "seq", None, None),
        P(),
        P(),
        P(),
        P(None, None, ("dp", "seq"), "tensor"),
        P(None, None, ("dp", "seq"), "tensor"),
        P(None, None, ("dp", "seq")),
        P(None, None, "tensor"),
        P(None, ("dp", "seq"), "tensor"),
        P(None, ("dp", "seq"), "tensor"),
        P(None, ("dp", "seq")),
        P(None, "tensor"),
        P(None, ("dp", "seq"), "tensor"),
        P(None, ("dp", "seq"), "tensor"),
        P(None, ("dp", "seq")),
        P(None, "tensor"),
    )
    sizes = dict(mesh.shape)
    fits = sizes["dp"] == 4 and sizes["seq"] == NZ and sizes["tensor"] == 2
    return jax.shard_map(
        per_device_kernels if fits else per_device, mesh=mesh, in_specs=in_specs, out_specs=out_specs, check_vma=False
    )
```
